32 devices in a mesh: groups: 2 (over y), obs: 4 (over z), cam: 4 (over x, core).
Axes of the slice: x: 2, y: 2, z: 4, core: 2. Of those that a mesh axis runs over, the one named last changes fastest.
Arguments:
- cameras: float32 [9, 1024], P(None, ('groups', 'cam')), parts along dimension 1, may hold values from -1 to 6, as said below
- points: float32 [3, 2048], P(None, ('groups', 'obs')), parts along dimension 1, may hold values from -1 to 1
- measured: float32 [256, 2, 128], P(('groups', 'obs', 'cam')), parts along dimension 0, may hold values from -1.5 to 1.5
- sqrt_weight: float32 [256, 128], P(('groups', 'obs', 'cam')), parts along dimension 0, may hold values from 0.5 to 2
- cam_index: int32 [256, 128], P(('groups', 'obs', 'cam')), parts along dimension 0, may hold values from 0 to 511
- point_slot: int32 [256, 128], P(('groups', 'obs', 'cam')), parts along dimension 0, may hold values from 0 to 255
- block_owner: int32 [256, 1], P(('groups', 'obs', 'cam')), parts along dimension 0, may hold values from 0 to 3; in each aligned block of 8 rows (0 to 7, 8 to 15, ...) at most 4 rows name the same one
- valid_count: int32 [256], P(('groups', 'obs', 'cam')), parts along dimension 0, may hold values from 32 to 128
Outputs:
- camera_step: float32 [9, 1024], P(None, ('groups', 'cam')), parts along dimension 1
- point_step: float32 [3, 2048], P(None, ('groups', 'obs')), parts along dimension 1
The draws below stay inside these ranges and needn't reach their ends.
There are 2 independent parts, one for each index of `groups`. The reference program is written for one: setup_inputs(seed, part) draws one part's arguments, and reference() takes and returns one part's arrays. A program takes and returns all parts, laid end to end along the dimension named above; each array names one. Nothing has to cross between parts.
Inputs may be any that keep to these rules, and one draw needn't show every extreme that they name: `cameras`: rows 0 to 2 lie in [-0.3, 0.3], rows 3 and 4 in [-1, 1], row 5 in [4, 6], row 6 in [0.5, 2], row 7 in [-0.2, 0.2], row 8 in [-0.1, 0.1]. `block_owner`: among the 8 rows of one device no shard is named by more than 4 rows, a bound that some block reaches.
All inputs are finite; a program needn't handle non-finite values.
Results may differ from the reference program's by a relative error of at most 0.0003.
Values sent between devices are 32-bit elements; how exact they have to be, the bound alone decides.
A program may use at most 64 MiB of HBM per device.

```python
import math
import jax
import jax.numpy as jnp
import numpy as np
from jax import lax

NBLK_DEV = 8
OBS_BLK = 128
PTS_DEV = 256
ITERS = 3
CAP = 4
BLOCKS = 128
CAMERAS = 512
POINTS = 1024
N_OBS = 4


def draw_cameras(key, part):
    key = jax.random.fold_in(key, 7)
    keys = jax.random.split(key, 6)
    rotation = jax.random.uniform(keys[0], (3, CAMERAS), jnp.float32, -0.3, 0.3)
    shift = jax.random.uniform(keys[1], (2, CAMERAS), jnp.float32, -1.0, 1.0)
    depth = jax.random.uniform(keys[2], (1, CAMERAS), jnp.float32, 4.0, 6.0)
    focal_len = 0.5 * 4.0 ** jax.random.uniform(keys[3], (1, CAMERAS), jnp.float32)
    radial_a = jax.random.uniform(keys[4], (1, CAMERAS), jnp.float32, -0.2, 0.2)
    radial_b = jax.random.uniform(keys[5], (1, CAMERAS), jnp.float32, -0.1, 0.1)
    return jnp.concatenate([rotation, shift, depth, focal_len, radial_a, radial_b], axis=0).astype(jnp.float32)


def with_ends(entries, key, low, top_value):
    longest = entries.shape.index(max(entries.shape))
    spots = []
    for shift in (0, 1):
        where = [jax.random.randint(jax.random.fold_in(key, axis), (), 0, length) for axis, length in enumerate(entries.shape)]
        where[longest] = (where[longest] + shift) % entries.shape[longest]
        spots.append(tuple(where))
    return entries.at[spots[0]].set(low).at[spots[1]].set(top_value)


def block_scale(stream_key, shape, shards, low, largest):
    loudness, own = 1.0, jax.random.fold_in(stream_key, 6)
    for position, shards_of in shards:
        draws = jnp.exp(jax.random.uniform(jax.random.fold_in(own, position), (shards_of,), jnp.float32, low / len(shards), largest / len(shards)))
        loudness = loudness * jnp.repeat(draws, shape[position] // shards_of).reshape([-1 if axis == position else 1 for axis in range(len(shape))])
    return loudness


def shared_out(key, own, number, rows, count, top, most, slope):
    sequence = jax.random.permutation(key, count)
    crowded, ordinary = shares(count, rows * top, most, slope, True), shares(count, rows * top, most, slope, False)
    places = jnp.arange(count)

    def named(tallies, offset_by):
        used = int((tallies > 0).sum())
        fixed = max(1, used // 4)
        moved = fixed + (places - fixed + offset_by * (used - fixed)) % max(1, count - fixed)
        return jnp.zeros((count,), jnp.int32).at[sequence[jnp.where(places < fixed, places, moved)]].set(jnp.asarray(tallies, jnp.int32))

    tallies = jnp.where(number % 4 == 0, named(crowded, number // 4), named(ordinary, number - number // 4 - 1))
    mixed = jax.random.permutation(jax.random.fold_in(own, 3), count)
    donor, receiver = mixed[0:count // 2 * 2:2], mixed[1:count // 2 * 2:2]
    room = jnp.minimum(tallies[donor] - 1, most - tallies[receiver]) // 2
    room = jnp.where((donor == sequence[0]) | (receiver == sequence[0]) | (tallies[receiver] == 0), 0, jnp.maximum(room, 0))
    moved = jax.random.randint(jax.random.fold_in(own, 4), (count // 2,), 0, 1 << 20) % (room + 1)
    tallies = tallies.at[donor].add(-moved).at[receiver].add(moved)
    items = jnp.searchsorted(jnp.cumsum(tallies), jnp.arange(rows * top), side="right").astype(jnp.int32)
    listing = items.reshape(top, rows).T
    listing = listing[jax.random.permutation(jax.random.fold_in(own, 1), rows)]
    offset_by = jax.random.randint(jax.random.fold_in(own, 2), (rows, 1), 0, top)
    return jnp.take_along_axis(listing, (jnp.arange(top)[None, :] + offset_by) % top, axis=1)


def shares(count, total, most, skew, full):
    weights = [(1 << 20) // math.isqrt(standing ** skew) + 1 for standing in range(1, count + 1)]
    largest = most if full else min(most, max(-(-total // count), total * weights[0] // sum(weights)))
    least = 1 if total - largest >= count - 1 else 0
    holding, spare = [largest] + [least] * (count - 1), total - largest - least * (count - 1)
    while spare > 0:
        free = [i for i in range(1, count) if holding[i] < largest] or [i for i in range(1, count) if holding[i] < most]
        mass, budget = sum([weights[i] for i in free]), spare
        for i in free:
            more = min(most - holding[i], max(1, budget * weights[i] // mass), spare)
            holding[i] = holding[i] + more
            spare = spare - more
    return np.array(holding)


def noise(key, dims, width, limit, pieces=(), dtype=jnp.bfloat16):
    drawn = width * jax.random.normal(key, dims, jnp.float32)
    if pieces:
        drawn = drawn * block_scale(key, dims, pieces, -0.22, 0.18)
    return jnp.clip(drawn, -limit, limit).astype(dtype)


def setup_inputs(seed: int = 0, part: int = 0) -> dict:
    seeds = jax.random.split(jax.random.key(seed), 9)
    part_keys = jax.random.split(jax.random.fold_in(seeds[8], part), 9)
    cameras = draw_cameras(jax.random.fold_in(jax.random.fold_in(seeds[8], part), 71), part)
    points = jnp.clip(jax.random.uniform(part_keys[1], (3, POINTS), jnp.float32, -1.0, 1.0) * block_scale(part_keys[1], (3, POINTS), ((1, 4),), -0.4, 0.0), -1.0, 1.0)
    measured = noise(part_keys[2], (BLOCKS, 2, OBS_BLK), 0.3, 1.5, ((0, 16),), jnp.float32)
    sqrt_weight = jnp.clip(jnp.exp(math.log(2.0) - 1.3862944 * jax.random.uniform(part_keys[3], (BLOCKS, OBS_BLK), jnp.float32) ** block_scale(part_keys[3], (BLOCKS, OBS_BLK), ((0, 16),), -0.2, 0.2)), 0.5, 2.0)
    cam_index = with_ends(jax.random.randint(part_keys[4], (BLOCKS, OBS_BLK), 0, CAMERAS), jax.random.fold_in(part_keys[4], 1), 0, CAMERAS - 1).astype(jnp.int32)
    point_slot = with_ends(jax.random.randint(part_keys[5], (BLOCKS, OBS_BLK), 0, PTS_DEV), jax.random.fold_in(part_keys[5], 1), 0, PTS_DEV - 1).astype(jnp.int32)
    block_owner_keys = jax.random.split(jax.random.fold_in(part_keys[6], 1), BLOCKS // NBLK_DEV)
    block_owner_turns = jax.random.permutation(jax.random.fold_in(part_keys[6], 3), BLOCKS // NBLK_DEV)
    block_owner = jax.vmap(lambda own, number: shared_out(jax.random.fold_in(part_keys[6], 2), own, number, NBLK_DEV, N_OBS, 1, CAP, 2))(block_owner_keys, block_owner_turns).reshape((BLOCKS, 1))
    valid_count = with_ends(jax.random.randint(part_keys[7], (BLOCKS,), 32, 129), jax.random.fold_in(part_keys[7], 1), 32, 128).astype(jnp.int32)
    return {"cameras": cameras, "points": points, "measured": measured, "sqrt_weight": sqrt_weight, "cam_index": cam_index, "point_slot": point_slot, "block_owner": block_owner, "valid_count": valid_count}


damping = 0.1
PAIR_LIST = ((9, 9), (9, 10), (9, 11), (10, 10), (10, 11), (11, 11))

def project(rot_a, rot_b, rot_c, move_a, move_b, move_c, focal_len, radial_a, radial_b, land_a, land_b, land_c):
    angle_sq = rot_a * rot_a + rot_b * rot_b + rot_c * rot_c
    first_coef = 1.0 - angle_sq / 6.0 + angle_sq * angle_sq / 120.0
    second_coef = 0.5 - angle_sq / 24.0 + angle_sq * angle_sq / 720.0
    cross_a = rot_b * land_c - rot_c * land_b
    cross_b = rot_c * land_a - rot_a * land_c
    cross_c = rot_a * land_b - rot_b * land_a
    twice_a = rot_b * cross_c - rot_c * cross_b
    twice_b = rot_c * cross_a - rot_a * cross_c
    twice_c = rot_a * cross_b - rot_b * cross_a
    frame_a = land_a + first_coef * cross_a + second_coef * twice_a + move_a
    frame_b = land_b + first_coef * cross_b + second_coef * twice_b + move_b
    frame_c = land_c + first_coef * cross_c + second_coef * twice_c + move_c
    plane_u = frame_a / frame_c
    plane_v = frame_b / frame_c
    radius_sq = plane_u * plane_u + plane_v * plane_v
    stretch = focal_len * (1.0 + radial_a * radius_sq + radial_b * radius_sq * radius_sq)
    return (stretch * plane_u, stretch * plane_v)

def linearize_residuals(model_parameters, measurement_u, measurement_v, robust_weighting):
    primals = tuple(model_parameters)
    entry_values, pullback = jax.vjp(project, *primals)
    all_ones = jnp.ones_like(entry_values[0])
    all_zeros = jnp.zeros_like(entry_values[0])
    grads_u = pullback((all_ones, all_zeros))
    grads_v = pullback((all_zeros, all_ones))
    slopes_u = [robust_weighting * member for member in grads_u]
    slopes_v = [robust_weighting * member for member in grads_v]
    residual_u = robust_weighting * (entry_values[0] - measurement_u)
    residual_v = robust_weighting * (entry_values[1] - measurement_v)
    return (residual_u, residual_v, slopes_u, slopes_v)

def solve_three(upper, right):
    minor_aa = upper[3] * upper[5] - upper[4] * upper[4]
    minor_ab = upper[2] * upper[4] - upper[1] * upper[5]
    minor_ac = upper[1] * upper[4] - upper[2] * upper[3]
    minor_bb = upper[0] * upper[5] - upper[2] * upper[2]
    minor_bc = upper[1] * upper[2] - upper[0] * upper[4]
    minor_cc = upper[0] * upper[3] - upper[1] * upper[1]
    determinant = upper[0] * minor_aa + upper[1] * minor_ab + upper[2] * minor_ac
    return ((minor_aa * right[0] + minor_ab * right[1] + minor_ac * right[2]) / determinant, (minor_ab * right[0] + minor_bb * right[1] + minor_bc * right[2]) / determinant, (minor_ac * right[0] + minor_bc * right[1] + minor_cc * right[2]) / determinant)

def reference(cameras, points, measured, sqrt_weight, cam_index, point_slot, block_owner, valid_count):
    lane_ids = lax.broadcasted_iota(jnp.int32, cam_index.shape, 1)
    in_use = (lane_ids < valid_count[:, None]).astype(jnp.float32)
    robust_weighting = (sqrt_weight * in_use).reshape(-1)
    flat_cam = cam_index.reshape(-1)
    flat_point = (block_owner[:, 0:1] * PTS_DEV + point_slot).reshape(-1)
    model_parameters = [cameras[member][flat_cam] for member in range(9)] + [points[member][flat_point] for member in range(3)]
    residual_u, residual_v, slopes_u, slopes_v = linearize_residuals(model_parameters, measured[:, 0, :].reshape(-1), measured[:, 1, :].reshape(-1), robust_weighting)

    def point_sum(summands):
        return [jax.ops.segment_sum(summand, flat_point, num_segments=POINTS) for summand in summands]

    def camera_sum(summands):
        return [jax.ops.segment_sum(summand, flat_cam, num_segments=CAMERAS) for summand in summands]

    def at_points(point_values):
        return [point_value[flat_point] for point_value in point_values]
    setup_rows = [slopes_u[first_pos] * slopes_u[second_pos] + slopes_v[first_pos] * slopes_v[second_pos] for first_pos, second_pos in PAIR_LIST]
    setup_rows += [slopes_u[9 + member] * residual_u + slopes_v[9 + member] * residual_v for member in range(3)]
    totals = point_sum(setup_rows)
    normal = tuple((totals[member] + damping if member in (0, 3, 5) else totals[member] for member in range(6)))
    gradient_pts = totals[6:]
    shifted = at_points(solve_three(normal, gradient_pts))
    back_u = sum((slopes_u[9 + member] * shifted[member] for member in range(3)))
    back_v = sum((slopes_v[9 + member] * shifted[member] for member in range(3)))
    cam_rows = [-(slopes_u[member] * residual_u + slopes_v[member] * residual_v) + slopes_u[member] * back_u + slopes_v[member] * back_v for member in range(9)]
    cam_rows += [slopes_u[member] * slopes_u[member] + slopes_v[member] * slopes_v[member] for member in range(9)]
    cam_totals = camera_sum(cam_rows)
    rhs = jnp.stack(cam_totals[:9])
    precond = jnp.stack(cam_totals[9:]) + damping

    def along_cameras(direction):
        at_obs = [direction[member][flat_cam] for member in range(9)]
        along_u = sum((slopes_u[member] * at_obs[member] for member in range(9)))
        along_v = sum((slopes_v[member] * at_obs[member] for member in range(9)))
        return (along_u, along_v)

    def apply_schur(direction):
        along_u, along_v = along_cameras(direction)
        pushed = point_sum([slopes_u[9 + member] * along_u + slopes_v[9 + member] * along_v for member in range(3)])
        pulled = at_points(solve_three(normal, pushed))
        left_u = along_u - sum((slopes_u[9 + member] * pulled[member] for member in range(3)))
        left_v = along_v - sum((slopes_v[9 + member] * pulled[member] for member in range(3)))
        summed = camera_sum([slopes_u[member] * left_u + slopes_v[member] * left_v for member in range(9)])
        return jnp.stack(summed) + damping * direction
    solution = jnp.zeros_like(rhs)
    residual = rhs
    scaled_res = residual / precond
    search = scaled_res
    inner = jnp.sum(residual * scaled_res)
    for step in range(ITERS):
        image = apply_schur(search)
        step_len = inner / jnp.sum(search * image)
        solution = solution + step_len * search
        residual = residual - step_len * image
        if step + 1 < ITERS:
            scaled_res = residual / precond
            inner_next = jnp.sum(residual * scaled_res)
            search = scaled_res + inner_next / inner * search
            inner = inner_next
    along_u, along_v = along_cameras(solution)
    pushed = point_sum([slopes_u[9 + member] * along_u + slopes_v[9 + member] * along_v for member in range(3)])
    update = solve_three(normal, [-(gradient_pts[member] + pushed[member]) for member in range(3)])
    return (solution, jnp.stack(update))
```

```python
import functools

import jax
import jax.numpy as jnp
from jax import lax
from jax.experimental import pallas as pl
from jax.experimental.pallas import tpu as pltpu
from jax.sharding import PartitionSpec as P

ITERS = 3
DAMPING = 0.1
PAIR_LIST = ((0, 0), (0, 1), (0, 2), (1, 1), (1, 2), (2, 2))
F32, BF16 = jnp.float32, jnp.bfloat16


def ceil_to(number, step):
    return -(-number // step) * step


def cross(a, b):
    return (a[1] * b[2] - a[2] * b[1], a[2] * b[0] - a[0] * b[2], a[0] * b[1] - a[1] * b[0])


def inner3(a, b):
    return a[0] * b[0] + a[1] * b[1] + a[2] * b[2]


def linearize(cam, point):
    w, t = cam[0:3], cam[3:6]
    focal, k1, k2 = cam[6], cam[7], cam[8]
    s = inner3(w, w)
    a = 1.0 - s / 6.0 + s * s / 120.0
    c = 0.5 - s / 24.0 + s * s / 720.0
    a_slope = -1.0 / 6.0 + s / 60.0
    c_slope = -1.0 / 24.0 + s / 360.0
    once = cross(w, point)
    twice = cross(w, once)
    frame = [point[i] + a * once[i] + c * twice[i] + t[i] for i in range(3)]
    inv = 1.0 / frame[2]
    u, v = frame[0] * inv, frame[1] * inv
    rho = u * u + v * v
    bend = 1.0 + k1 * rho + k2 * rho * rho
    bend_slope = k1 + 2.0 * k2 * rho
    scale = focal * inv
    uu = scale * (bend + 2.0 * u * u * bend_slope)
    uv = scale * (2.0 * u * v * bend_slope)
    vv = scale * (bend + 2.0 * v * v * bend_slope)
    grads = []
    for flat, g in ((u, (uu, uv, -(uu * u + uv * v))), (v, (uv, vv, -(uv * u + vv * v)))):
        along = 2.0 * (a_slope * inner3(g, once) + c_slope * inner3(g, twice))
        first, second, third = cross(point, g), cross(once, g), cross(point, cross(g, w))
        rot = [along * w[i] + a * first[i] + c * (second[i] + third[i]) for i in range(3)]
        wg = cross(w, g)
        wwg = cross(w, wg)
        land = [g[i] - a * wg[i] + c * wwg[i] for i in range(3)]
        fu = focal * rho * flat
        grads.append(rot + list(g) + [bend * flat, fu, fu * rho] + land)
    return focal * bend * u, focal * bend * v, grads[0], grads[1]


def pieces(x):
    high = x.astype(BF16)
    rest = x - high.astype(F32)
    mid = rest.astype(BF16)
    low = (rest - mid.astype(F32)).astype(BF16)
    return jnp.concatenate([high, mid, low], axis=0)


def joined(out):
    rows = out.shape[0] // 3
    return out[:rows] + (out[rows : 2 * rows] + out[2 * rows :])


def pad_rows(x, step):
    rows = x.shape[0]
    full = ceil_to(rows, step)
    if full == rows:
        return x
    return jnp.concatenate([x, jnp.zeros((full - rows, x.shape[1]), x.dtype)], axis=0)


def kernel(
    n_obs, n_cam,
    cameras, points, measured, weights, cam_index, point_slot, owner, valid,
    cam_out, point_out,
    cams_in, pts_in, setup_c, setup_o, pre_c, pre_o, push_c, push_o, sum_c, sum_o,
    cam_hot, pt_hot, slopes_u, slopes_v, full_x, full_p,
    send, recv,
):
    blocks, width = cam_index.shape
    slots = blocks * width
    pts_local = points.shape[1]
    cams_local = cameras.shape[1]
    cams_all = cams_local * n_cam
    chunks = cams_all // 128
    one = ceil_to(9 * chunks, 8)
    me = {"obs": lax.axis_index("obs"), "cam": lax.axis_index("cam")}
    size = {"obs": n_obs, "cam": n_cam}

    def partner(axis, step):
        return {axis: lax.rem(me[axis] + step, size[axis])}

    barrier = pltpu.get_barrier_semaphore()
    for axis in ("cam", "obs"):
        for step in range(1, size[axis]):
            pl.semaphore_signal(
                barrier, inc=1, device_id=partner(axis, step), device_id_type=pl.DeviceIdType.MESH
            )
    pl.semaphore_wait(barrier, n_obs + n_cam - 2)

    def begin(buf, number, axis):
        copies = []
        for step in range(1, size[axis]):
            copy = pltpu.make_async_remote_copy(
                src_ref=buf.at[me[axis]],
                dst_ref=buf.at[me[axis]],
                send_sem=send.at[number, step],
                recv_sem=recv.at[number, step],
                device_id=partner(axis, step),
                device_id_type=pl.DeviceIdType.MESH,
            )
            copy.start()
            copies.append(copy)
        return copies

    def finish(copies):
        for copy in copies:
            copy.wait()

    def total(buf, count):
        out = buf[0]
        for i in range(1, count):
            out = out + buf[i]
        return out

    def all_sum(first, second, number):
        finish(begin(first, number, "cam"))
        second[me["obs"]] = total(first, n_cam)
        finish(begin(second, number + 1, "obs"))
        return total(second, n_obs)

    cams_in[me["cam"]] = pad_rows(cameras[...], 16)
    pts_in[me["obs"]] = pad_rows(points[...], 8)
    copies = begin(cams_in, 0, "cam") + begin(pts_in, 1, "obs")

    def line(rows):
        return jnp.concatenate(rows, axis=1)

    cam_line = line([cam_index[b : b + 1, :] for b in range(blocks)])
    slot_line = line([point_slot[b : b + 1, :] for b in range(blocks)])
    owner_line = line([jnp.full((1, width), owner[b, 0], jnp.int32) for b in range(blocks)])
    meas_u = line([measured[b, 0:1, :] for b in range(blocks)])
    meas_v = line([measured[b, 1:2, :] for b in range(blocks)])
    lanes = lax.broadcasted_iota(jnp.int32, (1, width), 1)
    weight = line(
        [jnp.where(lanes < valid[b], weights[b : b + 1, :], 0.0) for b in range(blocks)]
    )
    for hot, index in ((cam_hot, cam_line), (pt_hot, slot_line)):
        for base in range(0, hot.shape[0], 128):
            ids = lax.broadcasted_iota(jnp.int32, (128, slots), 0) + base
            hot[base : base + 128, :] = jnp.where(ids == index, 1.0, 0.0).astype(BF16)
    mask = jnp.where(lax.broadcasted_iota(jnp.int32, (n_obs, slots), 0) == owner_line, 1.0, 0.0)

    def gather(x, hot):
        return joined(jnp.dot(pieces(x), hot[...], preferred_element_type=F32))

    def scatter(x, hot):
        return joined(
            lax.dot_general(
                pieces(x), hot[...], (((1,), (1,)), ((), ())), preferred_element_type=F32
            )
        )

    def to_points(rows):
        spread = jnp.concatenate([row * mask for row in rows], axis=0)
        return scatter(pad_rows(spread, 16), pt_hot)

    def from_points(members):
        got = gather(pad_rows(jnp.concatenate(members, axis=0), 16), pt_hot)
        return [
            jnp.sum(got[i * n_obs : (i + 1) * n_obs] * mask, axis=0, keepdims=True)
            for i in range(len(members))
        ]

    def members_of(table, count):
        return [table[i * n_obs : (i + 1) * n_obs] for i in range(count)]

    def pack(buf, vectors):
        for q, x in enumerate(vectors):
            for j in range(chunks):
                at, part = q * one + 8 * j, slice(128 * j, 128 * j + 128)
                buf[me["cam"], at : at + 8, :] = x[0:8, part]
                at = q * one + 8 * chunks + j
                buf[me["cam"], at : at + 1, :] = x[8:9, part]

    def unpack(table, q):
        base = q * one
        top = line([table[base + 8 * j : base + 8 * j + 8] for j in range(chunks)])
        base = base + 8 * chunks
        last = line([table[base + j : base + j + 1] for j in range(chunks)])
        return jnp.concatenate([top, last, jnp.zeros((7, cams_all), F32)], axis=0)

    pre_c[me["cam"]] = jnp.zeros(pre_c.shape[1:], F32)
    sum_c[me["cam"]] = jnp.zeros(sum_c.shape[1:], F32)
    finish(copies)

    params = gather(line([cams_in[j] for j in range(n_cam)]), cam_hot)
    places = from_points(
        [jnp.concatenate([pts_in[o, r : r + 1, :] for o in range(n_obs)], axis=0) for r in range(3)]
    )
    proj_u, proj_v, grads_u, grads_v = linearize([params[i : i + 1] for i in range(9)], places)
    resid_u, resid_v = weight * (proj_u - meas_u), weight * (proj_v - meas_v)
    for slopes, grads in ((slopes_u, grads_u), (slopes_v, grads_v)):
        slopes[...] = jnp.zeros_like(slopes)
        for i in range(9):
            slopes[i : i + 1, :] = weight * grads[i]
    land_u = [weight * grads_u[9 + i] for i in range(3)]
    land_v = [weight * grads_v[9 + i] for i in range(3)]

    rows = [land_u[i] * land_u[j] + land_v[i] * land_v[j] for i, j in PAIR_LIST]
    rows += [land_u[i] * resid_u + land_v[i] * resid_v for i in range(3)]
    setup_c[me["cam"]] = to_points(rows)
    totals = members_of(all_sum(setup_c, setup_o, 2), 9)
    full = [totals[i] + DAMPING if i in (0, 3, 5) else totals[i] for i in range(6)]
    gradient = totals[6:]
    minors = (
        full[3] * full[5] - full[4] * full[4],
        full[2] * full[4] - full[1] * full[5],
        full[1] * full[4] - full[2] * full[3],
        full[0] * full[5] - full[2] * full[2],
        full[1] * full[2] - full[0] * full[4],
        full[0] * full[3] - full[1] * full[1],
    )
    det = full[0] * minors[0] + full[1] * minors[1] + full[2] * minors[2]
    inverse = [minor / det for minor in minors]

    def solve(right):
        picks = ((0, 1, 2), (1, 3, 4), (2, 4, 5))
        return [sum(inverse[p[i]] * right[i] for i in range(3)) for p in picks]

    def at_slots(values):
        pulled = from_points(values)
        return inner3(land_u, pulled), inner3(land_v, pulled)

    back_u, back_v = at_slots(solve(gradient))
    ju, jv = slopes_u[...], slopes_v[...]
    both = scatter(
        jnp.concatenate(
            [ju * (back_u - resid_u) + jv * (back_v - resid_v), ju * ju + jv * jv], axis=0
        ),
        cam_hot,
    )
    pack(pre_c, [both[:16], both[16:]])
    table = all_sum(pre_c, pre_o, 4)
    rhs = unpack(table, 0)
    precond = unpack(table, 1) + DAMPING

    def push(x):
        at_obs = gather(x, cam_hot)
        along_u = jnp.sum(slopes_u[...] * at_obs, axis=0, keepdims=True)
        along_v = jnp.sum(slopes_v[...] * at_obs, axis=0, keepdims=True)
        push_c[me["cam"]] = to_points([land_u[i] * along_u + land_v[i] * along_v for i in range(3)])
        return along_u, along_v, members_of(all_sum(push_c, push_o, 6), 3)

    def dot(a, b):
        return jnp.sum(jnp.sum(a * b, axis=0, keepdims=True), axis=1, keepdims=True)

    def iterate(_, state):
        x, res, direction, rz = state
        along_u, along_v, pushed = push(direction)
        pulled_u, pulled_v = at_slots(solve(pushed))
        left_u, left_v = along_u - pulled_u, along_v - pulled_v
        pack(sum_c, [scatter(slopes_u[...] * left_u + slopes_v[...] * left_v, cam_hot)])
        image = unpack(all_sum(sum_c, sum_o, 8), 0) + DAMPING * direction
        alpha = rz / dot(direction, image)
        x = x + alpha * direction
        res = res - alpha * image
        pre = res / precond
        rz_new = dot(res, pre)
        return x, res, pre + (rz_new / rz) * direction, rz_new

    pre = rhs / precond
    state = (jnp.zeros_like(rhs), rhs, pre, dot(rhs, pre))
    x = lax.fori_loop(0, ITERS, iterate, state)[0]
    full_x[...] = x
    at = pl.multiple_of(me["cam"] * cams_local, cams_local)
    cam_out[...] = full_x[0:9, pl.ds(at, cams_local)]
    pushed = push(x)[2]
    steps = solve([-(gradient[i] + pushed[i]) for i in range(3)])
    for i in range(3):
        full_p[i] = steps[i]
        point_out[i : i + 1, :] = full_p[i, pl.ds(me["obs"], 1), :]


def local(cameras, points, measured, sqrt_weight, cam_index, point_slot, block_owner, valid_count):
    n_obs, n_cam = lax.axis_size("obs"), lax.axis_size("cam")
    slots = cam_index.shape[0] * cam_index.shape[1]
    pts_local, cams_local = points.shape[1], cameras.shape[1]
    cams_all = cams_local * n_cam
    one = ceil_to(9 * (cams_all // 128), 8)
    three, nine = ceil_to(3 * n_obs, 16), ceil_to(9 * n_obs, 16)

    def pair(rows, columns):
        return [pltpu.VMEM((count, rows, columns), F32) for count in (n_cam, n_obs)]

    vmem, smem = pl.BlockSpec(memory_space=pltpu.VMEM), pl.BlockSpec(memory_space=pltpu.SMEM)
    return pl.pallas_call(
        functools.partial(kernel, n_obs, n_cam),
        out_shape=(
            jax.ShapeDtypeStruct((9, cams_local), F32),
            jax.ShapeDtypeStruct((3, pts_local), F32),
        ),
        in_specs=[vmem] * 6 + [smem] * 2,
        out_specs=(vmem, vmem),
        scratch_shapes=[
            pltpu.VMEM((n_cam, 16, cams_local), F32),
            pltpu.VMEM((n_obs, 8, pts_local), F32),
            *pair(nine, pts_local),
            *pair(2 * one, 128),
            *pair(three, pts_local),
            *pair(one, 128),
            pltpu.VMEM((cams_all, slots), BF16),
            pltpu.VMEM((pts_local, slots), BF16),
            pltpu.VMEM((16, slots), F32),
            pltpu.VMEM((16, slots), F32),
            pltpu.VMEM((16, cams_all), F32),
            pltpu.VMEM((3, n_obs, pts_local), F32),
            pltpu.SemaphoreType.DMA((10, max(n_obs, n_cam))),
            pltpu.SemaphoreType.DMA((10, max(n_obs, n_cam))),
        ],
        compiler_params=pltpu.CompilerParams(
            collective_id=0, has_side_effects=True, vmem_limit_bytes=48 * 1024 * 1024
        ),
    )(cameras, points, measured, sqrt_weight, cam_index, point_slot, block_owner, valid_count)


def solution(mesh):
    return jax.shard_map(
        local,
        mesh=mesh,
        in_specs=(
            P(None, ("groups", "cam")),
            P(None, ("groups", "obs")),
            P(("groups", "obs", "cam"), None, None),
            P(("groups", "obs", "cam"), None),
            P(("groups", "obs", "cam"), None),
            P(("groups", "obs", "cam"), None),
            P(("groups", "obs", "cam"), None),
            P(("groups", "obs", "cam")),
        ),
        out_specs=(P(None, ("groups", "cam")), P(None, ("groups", "obs"))),
        check_vma=False,
    )
```

```python
import functools

import jax
import jax.numpy as jnp
from jax import lax
from jax.experimental import pallas as pl
from jax.experimental.pallas import tpu as pltpu
from jax.sharding import PartitionSpec as P

ITERS = 3
DAMPING = 0.1
PAIR_LIST = ((0, 0), (0, 1), (0, 2), (1, 1), (1, 2), (2, 2))
F32, BF16 = jnp.float32, jnp.bfloat16


def ceil_to(number, step):
    return -(-number // step) * step


def cross(a, b):
    return (a[1] * b[2] - a[2] * b[1], a[2] * b[0] - a[0] * b[2], a[0] * b[1] - a[1] * b[0])


def inner3(a, b):
    return a[0] * b[0] + a[1] * b[1] + a[2] * b[2]


def linearize(cam, point):
    w, t = cam[0:3], cam[3:6]
    focal, k1, k2 = cam[6], cam[7], cam[8]
    s = inner3(w, w)
    a = 1.0 - s / 6.0 + s * s / 120.0
    c = 0.5 - s / 24.0 + s * s / 720.0
    a_slope = -1.0 / 6.0 + s / 60.0
    c_slope = -1.0 / 24.0 + s / 360.0
    once = cross(w, point)
    twice = cross(w, once)
    frame = [point[i] + a * once[i] + c * twice[i] + t[i] for i in range(3)]
    inv = 1.0 / frame[2]
    u, v = frame[0] * inv, frame[1] * inv
    rho = u * u + v * v
    bend = 1.0 + k1 * rho + k2 * rho * rho
    bend_slope = k1 + 2.0 * k2 * rho
    scale = focal * inv
    uu = scale * (bend + 2.0 * u * u * bend_slope)
    uv = scale * (2.0 * u * v * bend_slope)
    vv = scale * (bend + 2.0 * v * v * bend_slope)
    grads = []
    for flat, g in ((u, (uu, uv, -(uu * u + uv * v))), (v, (uv, vv, -(uv * u + vv * v)))):
        along = 2.0 * (a_slope * inner3(g, once) + c_slope * inner3(g, twice))
        first, second, third = cross(point, g), cross(once, g), cross(point, cross(g, w))
        rot = [along * w[i] + a * first[i] + c * (second[i] + third[i]) for i in range(3)]
        wg = cross(w, g)
        wwg = cross(w, wg)
        land = [g[i] - a * wg[i] + c * wwg[i] for i in range(3)]
        fu = focal * rho * flat
        grads.append(rot + list(g) + [bend * flat, fu, fu * rho] + land)
    return focal * bend * u, focal * bend * v, grads[0], grads[1]


def pieces(x):
    high = x.astype(BF16)
    rest = x - high.astype(F32)
    mid = rest.astype(BF16)
    low = (rest - mid.astype(F32)).astype(BF16)
    return jnp.concatenate([high, mid, low], axis=0)


def joined(out):
    rows = out.shape[0] // 3
    return out[:rows] + (out[rows : 2 * rows] + out[2 * rows :])


def pad_rows(x, step):
    rows = x.shape[0]
    full = ceil_to(rows, step)
    if full == rows:
        return x
    return jnp.concatenate([x, jnp.zeros((full - rows, x.shape[1]), x.dtype)], axis=0)


def kernel(
    n_obs, n_cam,
    cameras, points, measured, weights, cam_index, point_slot, owner, valid,
    cam_out, point_out,
    cams_in, pts_in, setup_c, setup_o, pre_c, pre_o, push_c, push_o, sum_c, sum_o,
    cam_hot, pt_hot, slopes_u, slopes_v, full_x, full_p,
    send, recv,
):
    blocks, width = cam_index.shape
    slots = blocks * width
    pts_local = points.shape[1]
    cams_local = cameras.shape[1]
    cams_all = cams_local * n_cam
    chunks = cams_all // 128
    one = ceil_to(9 * chunks, 8)
    me = {"obs": lax.axis_index("obs"), "cam": lax.axis_index("cam")}
    size = {"obs": n_obs, "cam": n_cam}

    def partner(axis, step):
        return {axis: lax.rem(me[axis] + step, size[axis])}

    barrier = pltpu.get_barrier_semaphore()
    for axis in ("cam", "obs"):
        for step in range(1, size[axis]):
            pl.semaphore_signal(
                barrier, inc=1, device_id=partner(axis, step), device_id_type=pl.DeviceIdType.MESH
            )
    pl.semaphore_wait(barrier, n_obs + n_cam - 2)

    def begin(buf, number, axis):
        copies = []
        for step in range(1, size[axis]):
            copy = pltpu.make_async_remote_copy(
                src_ref=buf.at[me[axis]],
                dst_ref=buf.at[me[axis]],
                send_sem=send.at[number, step],
                recv_sem=recv.at[number, step],
                device_id=partner(axis, step),
                device_id_type=pl.DeviceIdType.MESH,
            )
            copy.start()
            copies.append(copy)
        return copies

    def finish(copies):
        for copy in copies:
            copy.wait()

    def total(buf, count):
        out = buf[0]
        for i in range(1, count):
            out = out + buf[i]
        return out

    def all_sum(first, second, number):
        finish(begin(first, number, "cam"))
        second[me["obs"]] = total(first, n_cam)
        finish(begin(second, number + 1, "obs"))
        return total(second, n_obs)

    cams_in[me["cam"]] = pad_rows(cameras[...], 16)
    pts_in[me["obs"]] = pad_rows(points[...], 8)
    copies = begin(cams_in, 0, "cam") + begin(pts_in, 1, "obs")

    def line(rows):
        return jnp.concatenate(rows, axis=1)

    cam_line = line([cam_index[b : b + 1, :] for b in range(blocks)])
    slot_line = line([point_slot[b : b + 1, :] for b in range(blocks)])
    owner_line = line([jnp.full((1, width), owner[b, 0], jnp.int32) for b in range(blocks)])
    meas_u = line([measured[b, 0:1, :] for b in range(blocks)])
    meas_v = line([measured[b, 1:2, :] for b in range(blocks)])
    lanes = lax.broadcasted_iota(jnp.int32, (1, width), 1)
    weight = line(
        [jnp.where(lanes < valid[b], weights[b : b + 1, :], 0.0) for b in range(blocks)]
    )
    for hot, index in ((cam_hot, cam_line), (pt_hot, slot_line)):
        for base in range(0, hot.shape[0], 128):
            ids = lax.broadcasted_iota(jnp.int32, (128, slots), 0) + base
            hot[base : base + 128, :] = jnp.where(ids == index, 1.0, 0.0).astype(BF16)
    mask = jnp.where(lax.broadcasted_iota(jnp.int32, (n_obs, slots), 0) == owner_line, 1.0, 0.0)

    def gather(x, hot):
        return joined(jnp.dot(pieces(x), hot[...], preferred_element_type=F32))

    def scatter(x, hot):
        return joined(
            lax.dot_general(
                pieces(x), hot[...], (((1,), (1,)), ((), ())), preferred_element_type=F32
            )
        )

    def to_points(rows):
        spread = jnp.concatenate([row * mask for row in rows], axis=0)
        return scatter(pad_rows(spread, 16), pt_hot)

    def from_points(members):
        got = gather(pad_rows(jnp.concatenate(members, axis=0), 16), pt_hot)
        return [
            jnp.sum(got[i * n_obs : (i + 1) * n_obs] * mask, axis=0, keepdims=True)
            for i in range(len(members))
        ]

    def members_of(table, count):
        return [table[i * n_obs : (i + 1) * n_obs] for i in range(count)]

    def pack(buf, vectors):
        for q, x in enumerate(vectors):
            for j in range(chunks):
                at, part = q * one + 8 * j, slice(128 * j, 128 * j + 128)
                buf[me["cam"], at : at + 8, :] = x[0:8, part]
                at = q * one + 8 * chunks + j
                buf[me["cam"], at : at + 1, :] = x[8:9, part]

    def unpack(table, q):
        base = q * one
        top = line([table[base + 8 * j : base + 8 * j + 8] for j in range(chunks)])
        base = base + 8 * chunks
        last = line([table[base + j : base + j + 1] for j in range(chunks)])
        return jnp.concatenate([top, last, jnp.zeros((7, cams_all), F32)], axis=0)

    pre_c[me["cam"]] = jnp.zeros(pre_c.shape[1:], F32)
    sum_c[me["cam"]] = jnp.zeros(sum_c.shape[1:], F32)
    finish(copies)

    params = gather(line([cams_in[j] for j in range(n_cam)]), cam_hot)
    places = from_points(
        [jnp.concatenate([pts_in[o, r : r + 1, :] for o in range(n_obs)], axis=0) for r in range(3)]
    )
    proj_u, proj_v, grads_u, grads_v = linearize([params[i : i + 1] for i in range(9)], places)
    resid_u, resid_v = weight * (proj_u - meas_u), weight * (proj_v - meas_v)
    for slopes, grads in ((slopes_u, grads_u), (slopes_v, grads_v)):
        slopes[...] = jnp.zeros_like(slopes)
        for i in range(9):
            slopes[i : i + 1, :] = weight * grads[i]
    land_u = [weight * grads_u[9 + i] for i in range(3)]
    land_v = [weight * grads_v[9 + i] for i in range(3)]

    rows = [land_u[i] * land_u[j] + land_v[i] * land_v[j] for i, j in PAIR_LIST]
    rows += [land_u[i] * resid_u + land_v[i] * resid_v for i in range(3)]
    setup_c[me["cam"]] = to_points(rows)
    totals = members_of(all_sum(setup_c, setup_o, 2), 9)
    full = [totals[i] + DAMPING if i in (0, 3, 5) else totals[i] for i in range(6)]
    gradient = totals[6:]
    minors = (
        full[3] * full[5] - full[4] * full[4],
        full[2] * full[4] - full[1] * full[5],
        full[1] * full[4] - full[2] * full[3],
        full[0] * full[5] - full[2] * full[2],
        full[1] * full[2] - full[0] * full[4],
        full[0] * full[3] - full[1] * full[1],
    )
    det = full[0] * minors[0] + full[1] * minors[1] + full[2] * minors[2]
    inverse = [minor / det for minor in minors]

    def solve(right):
        picks = ((0, 1, 2), (1, 3, 4), (2, 4, 5))
        return [sum(inverse[p[i]] * right[i] for i in range(3)) for p in picks]

    def at_slots(values):
        pulled = from_points(values)
        return inner3(land_u, pulled), inner3(land_v, pulled)

    back_u, back_v = at_slots(solve(gradient))
    ju, jv = slopes_u[...], slopes_v[...]
    both = scatter(
        jnp.concatenate(
            [ju * (back_u - resid_u) + jv * (back_v - resid_v), ju * ju + jv * jv], axis=0
        ),
        cam_hot,
    )
    pack(pre_c, [both[:16], both[16:]])
    table = all_sum(pre_c, pre_o, 4)
    rhs = unpack(table, 0)
    precond = unpack(table, 1) + DAMPING

    def push(x):
        at_obs = gather(x, cam_hot)
        along_u = jnp.sum(slopes_u[...] * at_obs, axis=0, keepdims=True)
        along_v = jnp.sum(slopes_v[...] * at_obs, axis=0, keepdims=True)
        push_c[me["cam"]] = to_points([land_u[i] * along_u + land_v[i] * along_v for i in range(3)])
        return along_u, along_v, members_of(all_sum(push_c, push_o, 6), 3)

    def dot(a, b):
        return jnp.sum(jnp.sum(a * b, axis=0, keepdims=True), axis=1, keepdims=True)

    def iterate(_, state):
        x, res, direction, rz, *sums = state
        along_u, along_v, pushed = push(direction)
        pulled_u, pulled_v = at_slots(solve(pushed))
        left_u, left_v = along_u - pulled_u, along_v - pulled_v
        pack(sum_c, [scatter(slopes_u[...] * left_u + slopes_v[...] * left_v, cam_hot)])
        image = unpack(all_sum(sum_c, sum_o, 8), 0) + DAMPING * direction
        alpha = rz / dot(direction, image)
        x = x + alpha * direction
        sums = [sums[i] + alpha * pushed[i] for i in range(3)]
        res = res - alpha * image
        pre = res / precond
        rz_new = dot(res, pre)
        return (x, res, pre + (rz_new / rz) * direction, rz_new, *sums)

    pre = rhs / precond
    sums = [jnp.zeros_like(gradient[0])] * 3
    state = (jnp.zeros_like(rhs), rhs, pre, dot(rhs, pre), *sums)
    x, _, _, _, *pushed = lax.fori_loop(0, ITERS, iterate, state)
    full_x[...] = x
    at = pl.multiple_of(me["cam"] * cams_local, cams_local)
    cam_out[...] = full_x[0:9, pl.ds(at, cams_local)]
    steps = solve([-(gradient[i] + pushed[i]) for i in range(3)])
    for i in range(3):
        full_p[i] = steps[i]
        point_out[i : i + 1, :] = full_p[i, pl.ds(me["obs"], 1), :]


def local(cameras, points, measured, sqrt_weight, cam_index, point_slot, block_owner, valid_count):
    n_obs, n_cam = lax.axis_size("obs"), lax.axis_size("cam")
    slots = cam_index.shape[0] * cam_index.shape[1]
    pts_local, cams_local = points.shape[1], cameras.shape[1]
    cams_all = cams_local * n_cam
    one = ceil_to(9 * (cams_all // 128), 8)
    three, nine = ceil_to(3 * n_obs, 16), ceil_to(9 * n_obs, 16)

    def pair(rows, columns):
        return [pltpu.VMEM((count, rows, columns), F32) for count in (n_cam, n_obs)]

    vmem, smem = pl.BlockSpec(memory_space=pltpu.VMEM), pl.BlockSpec(memory_space=pltpu.SMEM)
    return pl.pallas_call(
        functools.partial(kernel, n_obs, n_cam),
        out_shape=(
            jax.ShapeDtypeStruct((9, cams_local), F32),
            jax.ShapeDtypeStruct((3, pts_local), F32),
        ),
        in_specs=[vmem] * 6 + [smem] * 2,
        out_specs=(vmem, vmem),
        scratch_shapes=[
            pltpu.VMEM((n_cam, 16, cams_local), F32),
            pltpu.VMEM((n_obs, 8, pts_local), F32),
            *pair(nine, pts_local),
            *pair(2 * one, 128),
            *pair(three, pts_local),
            *pair(one, 128),
            pltpu.VMEM((cams_all, slots), BF16),
            pltpu.VMEM((pts_local, slots), BF16),
            pltpu.VMEM((16, slots), F32),
            pltpu.VMEM((16, slots), F32),
            pltpu.VMEM((16, cams_all), F32),
            pltpu.VMEM((3, n_obs, pts_local), F32),
            pltpu.SemaphoreType.DMA((10, max(n_obs, n_cam))),
            pltpu.SemaphoreType.DMA((10, max(n_obs, n_cam))),
        ],
        compiler_params=pltpu.CompilerParams(
            collective_id=0, has_side_effects=True, vmem_limit_bytes=48 * 1024 * 1024
        ),
    )(cameras, points, measured, sqrt_weight, cam_index, point_slot, block_owner, valid_count)


def solution(mesh):
    return jax.shard_map(
        local,
        mesh=mesh,
        in_specs=(
            P(None, ("groups", "cam")),
            P(None, ("groups", "obs")),
            P(("groups", "obs", "cam"), None, None),
            P(("groups", "obs", "cam"), None),
            P(("groups", "obs", "cam"), None),
            P(("groups", "obs", "cam"), None),
            P(("groups", "obs", "cam"), None),
            P(("groups", "obs", "cam")),
        ),
        out_specs=(P(None, ("groups", "cam")), P(None, ("groups", "obs"))),
        check_vma=False,
    )
```

```python
import functools

import jax
import jax.numpy as jnp
from jax import lax
from jax.experimental import pallas as pl
from jax.experimental.pallas import tpu as pltpu
from jax.sharding import PartitionSpec as P

ITERS = 3
DAMPING = 0.1
PAIR_LIST = ((0, 0), (0, 1), (0, 2), (1, 1), (1, 2), (2, 2))
F32, BF16 = jnp.float32, jnp.bfloat16


def ceil_to(number, step):
    return -(-number // step) * step


def cross(a, b):
    return (a[1] * b[2] - a[2] * b[1], a[2] * b[0] - a[0] * b[2], a[0] * b[1] - a[1] * b[0])


def inner3(a, b):
    return a[0] * b[0] + a[1] * b[1] + a[2] * b[2]


def linearize(cam, point):
    w, t = cam[0:3], cam[3:6]
    focal, k1, k2 = cam[6], cam[7], cam[8]
    s = inner3(w, w)
    a = 1.0 - s / 6.0 + s * s / 120.0
    c = 0.5 - s / 24.0 + s * s / 720.0
    a_slope = -1.0 / 6.0 + s / 60.0
    c_slope = -1.0 / 24.0 + s / 360.0
    once = cross(w, point)
    twice = cross(w, once)
    frame = [point[i] + a * once[i] + c * twice[i] + t[i] for i in range(3)]
    inv = 1.0 / frame[2]
    u, v = frame[0] * inv, frame[1] * inv
    rho = u * u + v * v
    bend = 1.0 + k1 * rho + k2 * rho * rho
    bend_slope = k1 + 2.0 * k2 * rho
    scale = focal * inv
    uu = scale * (bend + 2.0 * u * u * bend_slope)
    uv = scale * (2.0 * u * v * bend_slope)
    vv = scale * (bend + 2.0 * v * v * bend_slope)
    grads = []
    for flat, g in ((u, (uu, uv, -(uu * u + uv * v))), (v, (uv, vv, -(uv * u + vv * v)))):
        along = 2.0 * (a_slope * inner3(g, once) + c_slope * inner3(g, twice))
        first, second, third = cross(point, g), cross(once, g), cross(point, cross(g, w))
        rot = [along * w[i] + a * first[i] + c * (second[i] + third[i]) for i in range(3)]
        wg = cross(w, g)
        wwg = cross(w, wg)
        land = [g[i] - a * wg[i] + c * wwg[i] for i in range(3)]
        fu = focal * rho * flat
        grads.append(rot + list(g) + [bend * flat, fu, fu * rho] + land)
    return focal * bend * u, focal * bend * v, grads[0], grads[1]


def pieces(x):
    high = x.astype(BF16)
    rest = x - high.astype(F32)
    mid = rest.astype(BF16)
    low = (rest - mid.astype(F32)).astype(BF16)
    return jnp.concatenate([high, mid, low], axis=0)


def joined(out):
    rows = out.shape[0] // 3
    return out[:rows] + (out[rows : 2 * rows] + out[2 * rows :])


def pad_rows(x, step):
    rows = x.shape[0]
    full = ceil_to(rows, step)
    if full == rows:
        return x
    return jnp.concatenate([x, jnp.zeros((full - rows, x.shape[1]), x.dtype)], axis=0)


def kernel(
    n_obs, n_cam,
    cameras_in, points_in, measured_in, weights_in, cam_index_in, point_slot_in, owner, valid,
    cam_out, point_out,
    cams_in, pts_in, setup_c, setup_o, pre_c, pre_o, push_c, push_o, sum_c, sum_o,
    cam_hot, pt_hot, slopes_u, slopes_v, full_x, full_p,
    send, recv, load, cameras, points, measured, weights, cam_index, point_slot,
):
    blocks, width = cam_index.shape
    slots = blocks * width
    pts_local = points.shape[1]
    cams_local = cameras.shape[1]
    cams_all = cams_local * n_cam
    chunks = cams_all // 128
    one = ceil_to(9 * chunks, 8)
    me = {"obs": lax.axis_index("obs"), "cam": lax.axis_index("cam")}
    size = {"obs": n_obs, "cam": n_cam}

    def partner(axis, step):
        return {axis: lax.rem(me[axis] + step, size[axis])}

    sources = (cameras_in, points_in, measured_in, weights_in, cam_index_in, point_slot_in)
    targets = (cameras, points, measured, weights, cam_index, point_slot)
    loads = [pltpu.make_async_copy(a, b, load.at[i]) for i, (a, b) in enumerate(zip(sources, targets))]
    for copy in loads:
        copy.start()
    barrier = pltpu.get_barrier_semaphore()
    for axis in ("cam", "obs"):
        for step in range(1, size[axis]):
            pl.semaphore_signal(
                barrier, inc=1, device_id=partner(axis, step), device_id_type=pl.DeviceIdType.MESH
            )
    pl.semaphore_wait(barrier, n_obs + n_cam - 2)
    for copy in loads:
        copy.wait()

    def begin(buf, number, axis):
        copies = []
        for step in range(1, size[axis]):
            copy = pltpu.make_async_remote_copy(
                src_ref=buf.at[me[axis]],
                dst_ref=buf.at[me[axis]],
                send_sem=send.at[number, step],
                recv_sem=recv.at[number, step],
                device_id=partner(axis, step),
                device_id_type=pl.DeviceIdType.MESH,
            )
            copy.start()
            copies.append(copy)
        return copies

    def finish(copies):
        for copy in copies:
            copy.wait()

    def total(buf, count):
        out = buf[0]
        for i in range(1, count):
            out = out + buf[i]
        return out

    def all_sum(first, second, number):
        finish(begin(first, number, "cam"))
        second[me["obs"]] = total(first, n_cam)
        finish(begin(second, number + 1, "obs"))
        return total(second, n_obs)

    cams_in[me["cam"]] = pad_rows(cameras[...], 16)
    pts_in[me["obs"]] = pad_rows(points[...], 8)
    copies = begin(cams_in, 0, "cam") + begin(pts_in, 1, "obs")

    def line(rows):
        return jnp.concatenate(rows, axis=1)

    cam_line = line([cam_index[b : b + 1, :] for b in range(blocks)])
    slot_line = line([point_slot[b : b + 1, :] for b in range(blocks)])
    owner_line = line([jnp.broadcast_to(owner[b : b + 1, 0:1], (1, width)) for b in range(blocks)])
    meas_u = line([measured[b, 0:1, :] for b in range(blocks)])
    meas_v = line([measured[b, 1:2, :] for b in range(blocks)])
    lanes = lax.broadcasted_iota(jnp.int32, (1, width), 1)
    weight = line(
        [jnp.where(lanes < valid[b], weights[b : b + 1, :], 0.0) for b in range(blocks)]
    )
    for hot, index in ((cam_hot, cam_line), (pt_hot, slot_line)):
        for base in range(0, hot.shape[0], 128):
            ids = lax.broadcasted_iota(jnp.int32, (128, slots), 0) + base
            hot[base : base + 128, :] = jnp.where(ids == index, 1.0, 0.0).astype(BF16)
    mask = jnp.where(lax.broadcasted_iota(jnp.int32, (n_obs, slots), 0) == owner_line, 1.0, 0.0)

    def gather(x, hot):
        return joined(jnp.dot(pieces(x), hot[...], preferred_element_type=F32))

    def scatter(x, hot):
        return joined(
            lax.dot_general(
                pieces(x), hot[...], (((1,), (1,)), ((), ())), preferred_element_type=F32
            )
        )

    def to_points(rows):
        spread = jnp.concatenate([row * mask for row in rows], axis=0)
        return scatter(pad_rows(spread, 16), pt_hot)

    def from_points(members):
        got = gather(pad_rows(jnp.concatenate(members, axis=0), 16), pt_hot)
        return [
            jnp.sum(got[i * n_obs : (i + 1) * n_obs] * mask, axis=0, keepdims=True)
            for i in range(len(members))
        ]

    def members_of(table, count):
        return [table[i * n_obs : (i + 1) * n_obs] for i in range(count)]

    def pack(buf, vectors):
        for q, x in enumerate(vectors):
            for j in range(chunks):
                at, part = q * one + 8 * j, slice(128 * j, 128 * j + 128)
                buf[me["cam"], at : at + 8, :] = x[0:8, part]
                at = q * one + 8 * chunks + j
                buf[me["cam"], at : at + 1, :] = x[8:9, part]

    def unpack(table, q):
        base = q * one
        top = line([table[base + 8 * j : base + 8 * j + 8] for j in range(chunks)])
        base = base + 8 * chunks
        last = line([table[base + j : base + j + 1] for j in range(chunks)])
        return jnp.concatenate([top, last, jnp.zeros((7, cams_all), F32)], axis=0)

    pre_c[me["cam"]] = jnp.zeros(pre_c.shape[1:], F32)
    sum_c[me["cam"]] = jnp.zeros(sum_c.shape[1:], F32)
    finish(copies)

    params = gather(line([cams_in[j] for j in range(n_cam)]), cam_hot)
    places = from_points(
        [jnp.concatenate([pts_in[o, r : r + 1, :] for o in range(n_obs)], axis=0) for r in range(3)]
    )
    proj_u, proj_v, grads_u, grads_v = linearize([params[i : i + 1] for i in range(9)], places)
    resid_u, resid_v = weight * (proj_u - meas_u), weight * (proj_v - meas_v)
    for slopes, grads in ((slopes_u, grads_u), (slopes_v, grads_v)):
        slopes[...] = jnp.zeros_like(slopes)
        for i in range(9):
            slopes[i : i + 1, :] = weight * grads[i]
    land_u = [weight * grads_u[9 + i] for i in range(3)]
    land_v = [weight * grads_v[9 + i] for i in range(3)]

    rows = [land_u[i] * land_u[j] + land_v[i] * land_v[j] for i, j in PAIR_LIST]
    rows += [land_u[i] * resid_u + land_v[i] * resid_v for i in range(3)]
    setup_c[me["cam"]] = to_points(rows)[: setup_c.shape[1]]
    totals = members_of(all_sum(setup_c, setup_o, 2), 9)
    full = [totals[i] + DAMPING if i in (0, 3, 5) else totals[i] for i in range(6)]
    gradient = totals[6:]
    minors = (
        full[3] * full[5] - full[4] * full[4],
        full[2] * full[4] - full[1] * full[5],
        full[1] * full[4] - full[2] * full[3],
        full[0] * full[5] - full[2] * full[2],
        full[1] * full[2] - full[0] * full[4],
        full[0] * full[3] - full[1] * full[1],
    )
    det = full[0] * minors[0] + full[1] * minors[1] + full[2] * minors[2]
    inverse = [minor / det for minor in minors]

    def solve(right):
        picks = ((0, 1, 2), (1, 3, 4), (2, 4, 5))
        return [sum(inverse[p[i]] * right[i] for i in range(3)) for p in picks]

    def at_slots(values):
        pulled = from_points(values)
        return inner3(land_u, pulled), inner3(land_v, pulled)

    back_u, back_v = at_slots(solve(gradient))
    ju, jv = slopes_u[...], slopes_v[...]
    both = scatter(
        jnp.concatenate(
            [ju * (back_u - resid_u) + jv * (back_v - resid_v), ju * ju + jv * jv], axis=0
        ),
        cam_hot,
    )
    pack(pre_c, [both[:16], both[16:]])
    table = all_sum(pre_c, pre_o, 4)
    rhs = unpack(table, 0)
    precond = unpack(table, 1) + DAMPING

    def push(x):
        at_obs = gather(x, cam_hot)
        along_u = jnp.sum(slopes_u[...] * at_obs, axis=0, keepdims=True)
        along_v = jnp.sum(slopes_v[...] * at_obs, axis=0, keepdims=True)
        push_c[me["cam"]] = to_points([land_u[i] * along_u + land_v[i] * along_v for i in range(3)])
        return along_u, along_v, members_of(all_sum(push_c, push_o, 6), 3)

    def dot(a, b):
        return jnp.sum(jnp.sum(a * b, axis=0, keepdims=True), axis=1, keepdims=True)

    def iterate(_, state):
        x, res, direction, rz, *sums = state
        along_u, along_v, pushed = push(direction)
        pulled_u, pulled_v = at_slots(solve(pushed))
        left_u, left_v = along_u - pulled_u, along_v - pulled_v
        pack(sum_c, [scatter(slopes_u[...] * left_u + slopes_v[...] * left_v, cam_hot)])
        image = unpack(all_sum(sum_c, sum_o, 8), 0) + DAMPING * direction
        alpha = rz / dot(direction, image)
        x = x + alpha * direction
        sums = [sums[i] + alpha * pushed[i] for i in range(3)]
        res = res - alpha * image
        pre = res / precond
        rz_new = dot(res, pre)
        return (x, res, pre + (rz_new / rz) * direction, rz_new, *sums)

    pre = rhs / precond
    sums = [jnp.zeros_like(gradient[0])] * 3
    state = (jnp.zeros_like(rhs), rhs, pre, dot(rhs, pre), *sums)
    x, _, _, _, *pushed = lax.fori_loop(0, ITERS, iterate, state)
    full_x[...] = x
    at = pl.multiple_of(me["cam"] * cams_local, cams_local)
    cam_out[...] = full_x[0:9, pl.ds(at, cams_local)]
    steps = solve([-(gradient[i] + pushed[i]) for i in range(3)])
    for i in range(3):
        full_p[i] = steps[i]
        point_out[i : i + 1, :] = full_p[i, pl.ds(me["obs"], 1), :]


def local(cameras, points, measured, sqrt_weight, cam_index, point_slot, block_owner, valid_count):
    n_obs, n_cam = lax.axis_size("obs"), lax.axis_size("cam")
    slots = cam_index.shape[0] * cam_index.shape[1]
    pts_local, cams_local = points.shape[1], cameras.shape[1]
    cams_all = cams_local * n_cam
    one = ceil_to(9 * (cams_all // 128), 8)
    three, nine = ceil_to(3 * n_obs, 16), ceil_to(9 * n_obs, 8)

    def pair(rows, columns):
        return [pltpu.VMEM((count, rows, columns), F32) for count in (n_cam, n_obs)]

    vmem, smem = pl.BlockSpec(memory_space=pltpu.VMEM), pl.BlockSpec(memory_space=pltpu.SMEM)
    loaded = (cameras, points, measured, sqrt_weight, cam_index, point_slot)
    return pl.pallas_call(
        functools.partial(kernel, n_obs, n_cam),
        out_shape=(
            jax.ShapeDtypeStruct((9, cams_local), F32),
            jax.ShapeDtypeStruct((3, pts_local), F32),
        ),
        in_specs=[pl.BlockSpec(memory_space=pl.ANY)] * 6 + [vmem, smem],
        out_specs=(vmem, vmem),
        scratch_shapes=[
            pltpu.VMEM((n_cam, 16, cams_local), F32),
            pltpu.VMEM((n_obs, 8, pts_local), F32),
            *pair(nine, pts_local),
            *pair(2 * one, 128),
            *pair(three, pts_local),
            *pair(one, 128),
            pltpu.VMEM((cams_all, slots), BF16),
            pltpu.VMEM((pts_local, slots), BF16),
            pltpu.VMEM((16, slots), F32),
            pltpu.VMEM((16, slots), F32),
            pltpu.VMEM((16, cams_all), F32),
            pltpu.VMEM((3, n_obs, pts_local), F32),
            pltpu.SemaphoreType.DMA((10, max(n_obs, n_cam))),
            pltpu.SemaphoreType.DMA((10, max(n_obs, n_cam))),
            pltpu.SemaphoreType.DMA((6,)),
            *[pltpu.VMEM(x.shape, x.dtype) for x in loaded],
        ],
        compiler_params=pltpu.CompilerParams(
            collective_id=0, has_side_effects=True, vmem_limit_bytes=48 * 1024 * 1024
        ),
    )(cameras, points, measured, sqrt_weight, cam_index, point_slot, block_owner, valid_count)


def solution(mesh):
    return jax.shard_map(
        local,
        mesh=mesh,
        in_specs=(
            P(None, ("groups", "cam")),
            P(None, ("groups", "obs")),
            P(("groups", "obs", "cam"), None, None),
            P(("groups", "obs", "cam"), None),
            P(("groups", "obs", "cam"), None),
            P(("groups", "obs", "cam"), None),
            P(("groups", "obs", "cam"), None),
            P(("groups", "obs", "cam")),
        ),
        out_specs=(P(None, ("groups", "cam")), P(None, ("groups", "obs"))),
        check_vma=False,
    )
```

```python
import functools

import jax
import jax.numpy as jnp
from jax import lax
from jax.experimental import pallas as pl
from jax.experimental.pallas import tpu as pltpu
from jax.sharding import PartitionSpec as P

ITERS = 3
DAMPING = 0.1
PAIR_LIST = ((0, 0), (0, 1), (0, 2), (1, 1), (1, 2), (2, 2))
F32, BF16 = jnp.float32, jnp.bfloat16


def ceil_to(number, step):
    return -(-number // step) * step


def by_chips(n_obs, n_cam):
    return n_cam % 2 == 0 and n_obs * n_cam <= 16


def cross(a, b):
    return (a[1] * b[2] - a[2] * b[1], a[2] * b[0] - a[0] * b[2], a[0] * b[1] - a[1] * b[0])


def inner3(a, b):
    return a[0] * b[0] + a[1] * b[1] + a[2] * b[2]


def linearize(cam, point):
    w, t = cam[0:3], cam[3:6]
    focal, k1, k2 = cam[6], cam[7], cam[8]
    s = inner3(w, w)
    a = 1.0 - s / 6.0 + s * s / 120.0
    c = 0.5 - s / 24.0 + s * s / 720.0
    a_slope = -1.0 / 6.0 + s / 60.0
    c_slope = -1.0 / 24.0 + s / 360.0
    once = cross(w, point)
    twice = cross(w, once)
    frame = [point[i] + a * once[i] + c * twice[i] + t[i] for i in range(3)]
    inv = 1.0 / frame[2]
    u, v = frame[0] * inv, frame[1] * inv
    rho = u * u + v * v
    bend = 1.0 + k1 * rho + k2 * rho * rho
    bend_slope = k1 + 2.0 * k2 * rho
    scale = focal * inv
    uu = scale * (bend + 2.0 * u * u * bend_slope)
    uv = scale * (2.0 * u * v * bend_slope)
    vv = scale * (bend + 2.0 * v * v * bend_slope)
    grads = []
    for flat, g in ((u, (uu, uv, -(uu * u + uv * v))), (v, (uv, vv, -(uv * u + vv * v)))):
        along = 2.0 * (a_slope * inner3(g, once) + c_slope * inner3(g, twice))
        first, second, third = cross(point, g), cross(once, g), cross(point, cross(g, w))
        rot = [along * w[i] + a * first[i] + c * (second[i] + third[i]) for i in range(3)]
        wg = cross(w, g)
        wwg = cross(w, wg)
        land = [g[i] - a * wg[i] + c * wwg[i] for i in range(3)]
        fu = focal * rho * flat
        grads.append(rot + list(g) + [bend * flat, fu, fu * rho] + land)
    return focal * bend * u, focal * bend * v, grads[0], grads[1]


def pieces(x):
    high = x.astype(BF16)
    rest = x - high.astype(F32)
    mid = rest.astype(BF16)
    low = (rest - mid.astype(F32)).astype(BF16)
    return jnp.concatenate([high, mid, low], axis=0)


def joined(out):
    rows = out.shape[0] // 3
    return out[:rows] + (out[rows : 2 * rows] + out[2 * rows :])


def pad_rows(x, step):
    rows = x.shape[0]
    full = ceil_to(rows, step)
    if full == rows:
        return x
    return jnp.concatenate([x, jnp.zeros((full - rows, x.shape[1]), x.dtype)], axis=0)


def kernel(
    n_obs, n_cam,
    cameras_in, points_in, measured_in, weights_in, cam_index_in, point_slot_in, owner, valid,
    cam_out, point_out,
    cams_in, pts_in, setup_c, setup_o, setup_p, pre_c, pre_o, pre_p, push_c, push_o, push_p, sum_c, sum_o, sum_p,
    cam_hot, pt_hot, slopes_u, slopes_v, full_x, full_p,
    send, recv, load, cameras, points, measured, weights, cam_index, point_slot,
):
    blocks, width = cam_index.shape
    slots = blocks * width
    pts_local = points.shape[1]
    cams_local = cameras.shape[1]
    cams_all = cams_local * n_cam
    chunks = cams_all // 128
    one = ceil_to(9 * chunks, 8)
    me = {"obs": lax.axis_index("obs"), "cam": lax.axis_index("cam")}
    size = {"obs": n_obs, "cam": n_cam}

    flat, half = by_chips(n_obs, n_cam), n_cam // 2
    parity = lax.rem(me["cam"], 2)
    if flat:
        me.update(pair=parity, chips=me["obs"] * half + me["cam"] // 2)
        me.update(every=me["obs"] * n_cam + me["cam"])
        size.update(pair=2, chips=n_obs * half, every=n_obs * n_cam)
    lead = "pair" if flat else "cam"
    greeted = ("every",) if flat else ("cam", "obs")

    def partner(axis, step):
        other = lax.rem(me[axis] + step, size[axis])
        if axis == "pair":
            return {"cam": me["cam"] // 2 * 2 + other}
        if axis == "chips":
            return {"obs": other // half, "cam": lax.rem(other, half) * 2 + parity}
        if axis == "every":
            return {"obs": other // n_cam, "cam": lax.rem(other, n_cam)}
        return {axis: other}

    sources = (cameras_in, points_in, measured_in, weights_in, cam_index_in, point_slot_in)
    targets = (cameras, points, measured, weights, cam_index, point_slot)
    loads = [pltpu.make_async_copy(a, b, load.at[i]) for i, (a, b) in enumerate(zip(sources, targets))]
    for copy in loads:
        copy.start()
    barrier = pltpu.get_barrier_semaphore()
    for axis in greeted:
        for step in range(1, size[axis]):
            pl.semaphore_signal(
                barrier, inc=1, device_id=partner(axis, step), device_id_type=pl.DeviceIdType.MESH
            )
    pl.semaphore_wait(barrier, sum(size[axis] - 1 for axis in greeted))
    for copy in loads:
        copy.wait()

    def begin(buf, number, axis, rows=None):
        own = buf.at[me[axis]] if rows is None else buf.at[me[axis], rows]
        copies = []
        for step in range(1, size[axis]):
            copy = pltpu.make_async_remote_copy(
                src_ref=own,
                dst_ref=own,
                send_sem=send.at[number, step],
                recv_sem=recv.at[number, step],
                device_id=partner(axis, step),
                device_id_type=pl.DeviceIdType.MESH,
            )
            copy.start()
            copies.append(copy)
        return copies

    def finish(copies):
        for copy in copies:
            copy.wait()

    def total(buf, count):
        out = buf[0]
        for i in range(1, count):
            out = out + buf[i]
        return out

    def all_sum(first, second, third, number):
        if flat:
            rows = second.shape[1]
            mine = pl.ds(pl.multiple_of(parity * rows, 8), rows)
            theirs = pl.ds(pl.multiple_of((1 - parity) * rows, 8), rows)
            finish(begin(first, number, "pair", theirs))
            second[me["chips"]] = first[0, mine, :] + first[1, mine, :]
            finish(begin(second, number + 1, "chips"))
            third[parity] = total(second, size["chips"])
            finish(begin(third, number + 2, "pair"))
            return jnp.concatenate([third[0], third[1]], axis=0)
        finish(begin(first, number, "cam"))
        second[me["obs"]] = total(first, n_cam)
        finish(begin(second, number + 1, "obs"))
        return total(second, n_obs)

    cams_in[me["cam"]] = pad_rows(cameras[...], 16)
    pts_in[me["obs"]] = pad_rows(points[...], 8)
    copies = begin(cams_in, 0, "cam") + begin(pts_in, 1, "obs")

    def line(rows):
        return jnp.concatenate(rows, axis=1)

    cam_line = line([cam_index[b : b + 1, :] for b in range(blocks)])
    slot_line = line([point_slot[b : b + 1, :] for b in range(blocks)])
    owner_line = line([jnp.broadcast_to(owner[b : b + 1, 0:1], (1, width)) for b in range(blocks)])
    meas_u = line([measured[b, 0:1, :] for b in range(blocks)])
    meas_v = line([measured[b, 1:2, :] for b in range(blocks)])
    lanes = lax.broadcasted_iota(jnp.int32, (1, width), 1)
    weight = line(
        [jnp.where(lanes < valid[b], weights[b : b + 1, :], 0.0) for b in range(blocks)]
    )
    for hot, index in ((cam_hot, cam_line), (pt_hot, slot_line)):
        for base in range(0, hot.shape[0], 128):
            ids = lax.broadcasted_iota(jnp.int32, (128, slots), 0) + base
            hot[base : base + 128, :] = jnp.where(ids == index, 1.0, 0.0).astype(BF16)
    mask = jnp.where(lax.broadcasted_iota(jnp.int32, (n_obs, slots), 0) == owner_line, 1.0, 0.0)

    def gather(x, hot):
        return joined(jnp.dot(pieces(x), hot[...], preferred_element_type=F32))

    def scatter(x, hot):
        return joined(
            lax.dot_general(
                pieces(x), hot[...], (((1,), (1,)), ((), ())), preferred_element_type=F32
            )
        )

    def to_points(rows):
        spread = jnp.concatenate([row * mask for row in rows], axis=0)
        return scatter(pad_rows(spread, 16), pt_hot)

    def from_points(members):
        got = gather(pad_rows(jnp.concatenate(members, axis=0), 16), pt_hot)
        return [
            jnp.sum(got[i * n_obs : (i + 1) * n_obs] * mask, axis=0, keepdims=True)
            for i in range(len(members))
        ]

    def members_of(table, count):
        return [table[i * n_obs : (i + 1) * n_obs] for i in range(count)]

    def pack(buf, vectors):
        for q, x in enumerate(vectors):
            for j in range(chunks):
                at, part = q * one + 8 * j, slice(128 * j, 128 * j + 128)
                buf[me[lead], at : at + 8, :] = x[0:8, part]
                at = q * one + 8 * chunks + j
                buf[me[lead], at : at + 1, :] = x[8:9, part]

    def unpack(table, q):
        base = q * one
        top = line([table[base + 8 * j : base + 8 * j + 8] for j in range(chunks)])
        base = base + 8 * chunks
        last = line([table[base + j : base + j + 1] for j in range(chunks)])
        return jnp.concatenate([top, last, jnp.zeros((7, cams_all), F32)], axis=0)

    pre_c[me[lead]] = jnp.zeros(pre_c.shape[1:], F32)
    sum_c[me[lead]] = jnp.zeros(sum_c.shape[1:], F32)
    finish(copies)

    params = gather(line([cams_in[j] for j in range(n_cam)]), cam_hot)
    places = from_points(
        [jnp.concatenate([pts_in[o, r : r + 1, :] for o in range(n_obs)], axis=0) for r in range(3)]
    )
    proj_u, proj_v, grads_u, grads_v = linearize([params[i : i + 1] for i in range(9)], places)
    resid_u, resid_v = weight * (proj_u - meas_u), weight * (proj_v - meas_v)
    for slopes, grads in ((slopes_u, grads_u), (slopes_v, grads_v)):
        slopes[...] = jnp.zeros_like(slopes)
        for i in range(9):
            slopes[i : i + 1, :] = weight * grads[i]
    land_u = [weight * grads_u[9 + i] for i in range(3)]
    land_v = [weight * grads_v[9 + i] for i in range(3)]

    rows = [land_u[i] * land_u[j] + land_v[i] * land_v[j] for i, j in PAIR_LIST]
    rows += [land_u[i] * resid_u + land_v[i] * resid_v for i in range(3)]
    setup_c[me[lead]] = to_points(rows)[: setup_c.shape[1]]
    totals = members_of(all_sum(setup_c, setup_o, setup_p, 2), 9)
    full = [totals[i] + DAMPING if i in (0, 3, 5) else totals[i] for i in range(6)]
    gradient = totals[6:]
    minors = (
        full[3] * full[5] - full[4] * full[4],
        full[2] * full[4] - full[1] * full[5],
        full[1] * full[4] - full[2] * full[3],
        full[0] * full[5] - full[2] * full[2],
        full[1] * full[2] - full[0] * full[4],
        full[0] * full[3] - full[1] * full[1],
    )
    det = full[0] * minors[0] + full[1] * minors[1] + full[2] * minors[2]
    inverse = [minor / det for minor in minors]

    def solve(right):
        picks = ((0, 1, 2), (1, 3, 4), (2, 4, 5))
        return [sum(inverse[p[i]] * right[i] for i in range(3)) for p in picks]

    def at_slots(values):
        pulled = from_points(values)
        return inner3(land_u, pulled), inner3(land_v, pulled)

    back_u, back_v = at_slots(solve(gradient))
    ju, jv = slopes_u[...], slopes_v[...]
    both = scatter(
        jnp.concatenate(
            [ju * (back_u - resid_u) + jv * (back_v - resid_v), ju * ju + jv * jv], axis=0
        ),
        cam_hot,
    )
    pack(pre_c, [both[:16], both[16:]])
    table = all_sum(pre_c, pre_o, pre_p, 5)
    rhs = unpack(table, 0)
    precond = unpack(table, 1) + DAMPING

    def push(x):
        at_obs = gather(x, cam_hot)
        along_u = jnp.sum(slopes_u[...] * at_obs, axis=0, keepdims=True)
        along_v = jnp.sum(slopes_v[...] * at_obs, axis=0, keepdims=True)
        push_c[me[lead]] = to_points([land_u[i] * along_u + land_v[i] * along_v for i in range(3)])
        return along_u, along_v, members_of(all_sum(push_c, push_o, push_p, 8), 3)

    def dot(a, b):
        return jnp.sum(jnp.sum(a * b, axis=0, keepdims=True), axis=1, keepdims=True)

    def iterate(_, state):
        x, res, direction, rz, *sums = state
        along_u, along_v, pushed = push(direction)
        pulled_u, pulled_v = at_slots(solve(pushed))
        left_u, left_v = along_u - pulled_u, along_v - pulled_v
        pack(sum_c, [scatter(slopes_u[...] * left_u + slopes_v[...] * left_v, cam_hot)])
        image = unpack(all_sum(sum_c, sum_o, sum_p, 11), 0) + DAMPING * direction
        alpha = rz / dot(direction, image)
        x = x + alpha * direction
        sums = [sums[i] + alpha * pushed[i] for i in range(3)]
        res = res - alpha * image
        pre = res / precond
        rz_new = dot(res, pre)
        return (x, res, pre + (rz_new / rz) * direction, rz_new, *sums)

    pre = rhs / precond
    sums = [jnp.zeros_like(gradient[0])] * 3
    state = (jnp.zeros_like(rhs), rhs, pre, dot(rhs, pre), *sums)
    x, _, _, _, *pushed = lax.fori_loop(0, ITERS, iterate, state)
    full_x[...] = x
    at = pl.multiple_of(me["cam"] * cams_local, cams_local)
    cam_out[...] = full_x[0:9, pl.ds(at, cams_local)]
    steps = solve([-(gradient[i] + pushed[i]) for i in range(3)])
    for i in range(3):
        full_p[i] = steps[i]
        point_out[i : i + 1, :] = full_p[i, pl.ds(me["obs"], 1), :]


def local(cameras, points, measured, sqrt_weight, cam_index, point_slot, block_owner, valid_count):
    n_obs, n_cam = lax.axis_size("obs"), lax.axis_size("cam")
    slots = cam_index.shape[0] * cam_index.shape[1]
    pts_local, cams_local = points.shape[1], cameras.shape[1]
    cams_all = cams_local * n_cam
    one = ceil_to(9 * (cams_all // 128), 8)
    three, nine = ceil_to(3 * n_obs, 16), ceil_to(9 * n_obs, 16)

    flat, chips = by_chips(n_obs, n_cam), n_obs * n_cam // 2

    def pair(rows, columns):
        if not flat:
            return [pltpu.VMEM((n, rows, columns), F32) for n in (n_cam, n_obs)] + [
                pltpu.VMEM((1, 8, 128), F32)
            ]
        part = rows // 2
        return [
            pltpu.VMEM((2, rows, columns), F32),
            pltpu.VMEM((chips, part, columns), F32),
            pltpu.VMEM((2, part, columns), F32),
        ]

    vmem, smem = pl.BlockSpec(memory_space=pltpu.VMEM), pl.BlockSpec(memory_space=pltpu.SMEM)
    loaded = (cameras, points, measured, sqrt_weight, cam_index, point_slot)
    return pl.pallas_call(
        functools.partial(kernel, n_obs, n_cam),
        out_shape=(
            jax.ShapeDtypeStruct((9, cams_local), F32),
            jax.ShapeDtypeStruct((3, pts_local), F32),
        ),
        in_specs=[pl.BlockSpec(memory_space=pl.ANY)] * 6 + [vmem, smem],
        out_specs=(vmem, vmem),
        scratch_shapes=[
            pltpu.VMEM((n_cam, 16, cams_local), F32),
            pltpu.VMEM((n_obs, 8, pts_local), F32),
            *pair(nine, pts_local),
            *pair(2 * one, 128),
            *pair(three, pts_local),
            *pair(ceil_to(one, 16), 128),
            pltpu.VMEM((cams_all, slots), BF16),
            pltpu.VMEM((pts_local, slots), BF16),
            pltpu.VMEM((16, slots), F32),
            pltpu.VMEM((16, slots), F32),
            pltpu.VMEM((16, cams_all), F32),
            pltpu.VMEM((3, n_obs, pts_local), F32),
            pltpu.SemaphoreType.DMA((14, max(n_obs, n_cam, chips if flat else 0))),
            pltpu.SemaphoreType.DMA((14, max(n_obs, n_cam, chips if flat else 0))),
            pltpu.SemaphoreType.DMA((6,)),
            *[pltpu.VMEM(x.shape, x.dtype) for x in loaded],
        ],
        compiler_params=pltpu.CompilerParams(
            collective_id=0, has_side_effects=True, vmem_limit_bytes=48 * 1024 * 1024
        ),
    )(cameras, points, measured, sqrt_weight, cam_index, point_slot, block_owner, valid_count)


def solution(mesh):
    return jax.shard_map(
        local,
        mesh=mesh,
        in_specs=(
            P(None, ("groups", "cam")),
            P(None, ("groups", "obs")),
            P(("groups", "obs", "cam"), None, None),
            P(("groups", "obs", "cam"), None),
            P(("groups", "obs", "cam"), None),
            P(("groups", "obs", "cam"), None),
            P(("groups", "obs", "cam"), None),
            P(("groups", "obs", "cam")),
        ),
        out_specs=(P(None, ("groups", "cam")), P(None, ("groups", "obs"))),
        check_vma=False,
    )
```

```python
import functools

import jax
import jax.numpy as jnp
from jax import lax
from jax.experimental import pallas as pl
from jax.experimental.pallas import tpu as pltpu
from jax.sharding import PartitionSpec as P

ITERS = 3
DAMPING = 0.1
PAIR_LIST = ((0, 0), (0, 1), (0, 2), (1, 1), (1, 2), (2, 2))
F32, BF16 = jnp.float32, jnp.bfloat16


def ceil_to(number, step):
    return -(-number // step) * step


def by_chips(n_obs, n_cam):
    return n_cam % 2 == 0 and n_obs * n_cam <= 16


def cross(a, b):
    return (a[1] * b[2] - a[2] * b[1], a[2] * b[0] - a[0] * b[2], a[0] * b[1] - a[1] * b[0])


def inner3(a, b):
    return a[0] * b[0] + a[1] * b[1] + a[2] * b[2]


def linearize(cam, point):
    w, t = cam[0:3], cam[3:6]
    focal, k1, k2 = cam[6], cam[7], cam[8]
    s = inner3(w, w)
    a = 1.0 - s / 6.0 + s * s / 120.0
    c = 0.5 - s / 24.0 + s * s / 720.0
    a_slope = -1.0 / 6.0 + s / 60.0
    c_slope = -1.0 / 24.0 + s / 360.0
    once = cross(w, point)
    twice = cross(w, once)
    frame = [point[i] + a * once[i] + c * twice[i] + t[i] for i in range(3)]
    inv = 1.0 / frame[2]
    u, v = frame[0] * inv, frame[1] * inv
    rho = u * u + v * v
    bend = 1.0 + k1 * rho + k2 * rho * rho
    bend_slope = k1 + 2.0 * k2 * rho
    scale = focal * inv
    uu = scale * (bend + 2.0 * u * u * bend_slope)
    uv = scale * (2.0 * u * v * bend_slope)
    vv = scale * (bend + 2.0 * v * v * bend_slope)
    grads = []
    for flat, g in ((u, (uu, uv, -(uu * u + uv * v))), (v, (uv, vv, -(uv * u + vv * v)))):
        along = 2.0 * (a_slope * inner3(g, once) + c_slope * inner3(g, twice))
        first, second, third = cross(point, g), cross(once, g), cross(point, cross(g, w))
        rot = [along * w[i] + a * first[i] + c * (second[i] + third[i]) for i in range(3)]
        wg = cross(w, g)
        wwg = cross(w, wg)
        land = [g[i] - a * wg[i] + c * wwg[i] for i in range(3)]
        fu = focal * rho * flat
        grads.append(rot + list(g) + [bend * flat, fu, fu * rho] + land)
    return focal * bend * u, focal * bend * v, grads[0], grads[1]


def pieces(x):
    high = x.astype(BF16)
    rest = x - high.astype(F32)
    mid = rest.astype(BF16)
    low = (rest - mid.astype(F32)).astype(BF16)
    return jnp.concatenate([high, mid, low], axis=0)


def joined(out):
    rows = out.shape[0] // 3
    return out[:rows] + (out[rows : 2 * rows] + out[2 * rows :])


def pad_rows(x, step):
    rows = x.shape[0]
    full = ceil_to(rows, step)
    if full == rows:
        return x
    return jnp.concatenate([x, jnp.zeros((full - rows, x.shape[1]), x.dtype)], axis=0)


def kernel(
    n_obs, n_cam,
    cameras_in, points_in, measured_in, weights_in, cam_index_in, point_slot_in, owner, valid,
    cam_out, point_out,
    cams_in, pts_in, setup_c, setup_o, setup_p, pre_c, pre_o, pre_p, push_c, push_o, push_p, sum_c, sum_o, sum_p,
    cam_hot, pt_hot, slopes_u, slopes_v, full_x, full_p,
    send, recv, load, cameras, points, measured, weights, cam_index, point_slot,
):
    blocks, width = cam_index.shape
    slots = blocks * width
    pts_local = points.shape[1]
    cams_local = cameras.shape[1]
    cams_all = cams_local * n_cam
    chunks = cams_all // 128
    one = ceil_to(9 * chunks, 8)
    me = {"obs": lax.axis_index("obs"), "cam": lax.axis_index("cam")}
    size = {"obs": n_obs, "cam": n_cam}

    flat, half = by_chips(n_obs, n_cam), n_cam // 2
    parity = lax.rem(me["cam"], 2)
    if flat:
        me.update(pair=parity, chips=me["obs"] * half + me["cam"] // 2)
        me.update(every=me["obs"] * n_cam + me["cam"])
        size.update(pair=2, chips=n_obs * half, every=n_obs * n_cam)
    lead = "pair" if flat else "cam"
    greeted = ("every",) if flat else ("cam", "obs")

    def partner(axis, step):
        other = lax.rem(me[axis] + step, size[axis])
        if axis == "pair":
            return {"cam": me["cam"] // 2 * 2 + other}
        if axis == "chips":
            return {"obs": other // half, "cam": lax.rem(other, half) * 2 + parity}
        if axis == "every":
            return {"obs": other // n_cam, "cam": lax.rem(other, n_cam)}
        return {axis: other}

    sources = (cameras_in, points_in, measured_in, weights_in, cam_index_in, point_slot_in)
    targets = (cameras, points, measured, weights, cam_index, point_slot)
    loads = [pltpu.make_async_copy(a, b, load.at[i]) for i, (a, b) in enumerate(zip(sources, targets))]
    for copy in loads:
        copy.start()
    barrier = pltpu.get_barrier_semaphore()
    for axis in greeted:
        for step in range(1, size[axis]):
            pl.semaphore_signal(
                barrier, inc=1, device_id=partner(axis, step), device_id_type=pl.DeviceIdType.MESH
            )
    pl.semaphore_wait(barrier, sum(size[axis] - 1 for axis in greeted))
    for copy in loads:
        copy.wait()

    def begin(buf, number, axis, rows=None):
        own = buf.at[me[axis]] if rows is None else buf.at[me[axis], rows]
        copies = []
        for step in range(1, size[axis]):
            copy = pltpu.make_async_remote_copy(
                src_ref=own,
                dst_ref=own,
                send_sem=send.at[number, step],
                recv_sem=recv.at[number, step],
                device_id=partner(axis, step),
                device_id_type=pl.DeviceIdType.MESH,
            )
            copy.start()
            copies.append(copy)
        return copies

    sending = []

    def sent():
        while sending:
            sending.pop().wait_send()

    def finish(copies):
        for copy in copies:
            copy.wait_recv()
        sending.extend(copies)

    def total(buf, count):
        out = buf[0]
        for i in range(1, count):
            out = out + buf[i]
        return out

    def all_sum(first, second, third, number):
        if flat:
            rows = second.shape[1]
            mine = pl.ds(pl.multiple_of(parity * rows, 8), rows)
            theirs = pl.ds(pl.multiple_of((1 - parity) * rows, 8), rows)
            finish(begin(first, number, "pair", theirs))
            second[me["chips"]] = first[0, mine, :] + first[1, mine, :]
            finish(begin(second, number + 1, "chips"))
            third[parity] = total(second, size["chips"])
            copies = begin(third, number + 2, "pair")
            sent()
            finish(copies)
            return jnp.concatenate([third[0], third[1]], axis=0)
        finish(begin(first, number, "cam"))
        second[me["obs"]] = total(first, n_cam)
        finish(begin(second, number + 1, "obs"))
        return total(second, n_obs)

    cams_in[me["cam"]] = pad_rows(cameras[...], 16)
    pts_in[me["obs"]] = pad_rows(points[...], 8)
    copies = begin(cams_in, 0, "cam") + begin(pts_in, 1, "obs")

    def line(rows):
        return jnp.concatenate(rows, axis=1)

    cam_line = line([cam_index[b : b + 1, :] for b in range(blocks)])
    slot_line = line([point_slot[b : b + 1, :] for b in range(blocks)])
    owner_line = line([jnp.broadcast_to(owner[b : b + 1, 0:1], (1, width)) for b in range(blocks)])
    meas_u = line([measured[b, 0:1, :] for b in range(blocks)])
    meas_v = line([measured[b, 1:2, :] for b in range(blocks)])
    lanes = lax.broadcasted_iota(jnp.int32, (1, width), 1)
    weight = line(
        [jnp.where(lanes < valid[b], weights[b : b + 1, :], 0.0) for b in range(blocks)]
    )
    for hot, index in ((cam_hot, cam_line), (pt_hot, slot_line)):
        for base in range(0, hot.shape[0], 128):
            ids = lax.broadcasted_iota(jnp.int32, (128, slots), 0) + base
            hot[base : base + 128, :] = jnp.where(ids == index, 1.0, 0.0).astype(BF16)
    mask = jnp.where(lax.broadcasted_iota(jnp.int32, (n_obs, slots), 0) == owner_line, 1.0, 0.0)

    def gather(x, hot):
        return joined(jnp.dot(pieces(x), hot[...], preferred_element_type=F32))

    def scatter(x, hot):
        return joined(
            lax.dot_general(
                pieces(x), hot[...], (((1,), (1,)), ((), ())), preferred_element_type=F32
            )
        )

    def to_points(rows):
        spread = jnp.concatenate([row * mask for row in rows], axis=0)
        return scatter(pad_rows(spread, 16), pt_hot)

    def from_points(members):
        got = gather(pad_rows(jnp.concatenate(members, axis=0), 16), pt_hot)
        return [
            jnp.sum(got[i * n_obs : (i + 1) * n_obs] * mask, axis=0, keepdims=True)
            for i in range(len(members))
        ]

    def members_of(table, count):
        return [table[i * n_obs : (i + 1) * n_obs] for i in range(count)]

    def pack(buf, vectors):
        for q, x in enumerate(vectors):
            for j in range(chunks):
                at, part = q * one + 8 * j, slice(128 * j, 128 * j + 128)
                buf[me[lead], at : at + 8, :] = x[0:8, part]
                at = q * one + 8 * chunks + j
                buf[me[lead], at : at + 1, :] = x[8:9, part]

    def unpack(table, q):
        base = q * one
        top = line([table[base + 8 * j : base + 8 * j + 8] for j in range(chunks)])
        base = base + 8 * chunks
        last = line([table[base + j : base + j + 1] for j in range(chunks)])
        return jnp.concatenate([top, last, jnp.zeros((7, cams_all), F32)], axis=0)

    pre_c[me[lead]] = jnp.zeros(pre_c.shape[1:], F32)
    sum_c[me[lead]] = jnp.zeros(sum_c.shape[1:], F32)
    finish(copies)

    params = gather(line([cams_in[j] for j in range(n_cam)]), cam_hot)
    places = from_points(
        [jnp.concatenate([pts_in[o, r : r + 1, :] for o in range(n_obs)], axis=0) for r in range(3)]
    )
    proj_u, proj_v, grads_u, grads_v = linearize([params[i : i + 1] for i in range(9)], places)
    resid_u, resid_v = weight * (proj_u - meas_u), weight * (proj_v - meas_v)
    for slopes, grads in ((slopes_u, grads_u), (slopes_v, grads_v)):
        slopes[...] = jnp.zeros_like(slopes)
        for i in range(9):
            slopes[i : i + 1, :] = weight * grads[i]
    land_u = [weight * grads_u[9 + i] for i in range(3)]
    land_v = [weight * grads_v[9 + i] for i in range(3)]

    rows = [land_u[i] * land_u[j] + land_v[i] * land_v[j] for i, j in PAIR_LIST]
    rows += [land_u[i] * resid_u + land_v[i] * resid_v for i in range(3)]
    setup_c[me[lead]] = to_points(rows)[: setup_c.shape[1]]
    totals = members_of(all_sum(setup_c, setup_o, setup_p, 2), 9)
    full = [totals[i] + DAMPING if i in (0, 3, 5) else totals[i] for i in range(6)]
    gradient = totals[6:]
    minors = (
        full[3] * full[5] - full[4] * full[4],
        full[2] * full[4] - full[1] * full[5],
        full[1] * full[4] - full[2] * full[3],
        full[0] * full[5] - full[2] * full[2],
        full[1] * full[2] - full[0] * full[4],
        full[0] * full[3] - full[1] * full[1],
    )
    det = full[0] * minors[0] + full[1] * minors[1] + full[2] * minors[2]
    inverse = [minor / det for minor in minors]

    def solve(right):
        picks = ((0, 1, 2), (1, 3, 4), (2, 4, 5))
        return [sum(inverse[p[i]] * right[i] for i in range(3)) for p in picks]

    def at_slots(values):
        pulled = from_points(values)
        return inner3(land_u, pulled), inner3(land_v, pulled)

    back_u, back_v = at_slots(solve(gradient))
    ju, jv = slopes_u[...], slopes_v[...]
    both = scatter(
        jnp.concatenate(
            [ju * (back_u - resid_u) + jv * (back_v - resid_v), ju * ju + jv * jv], axis=0
        ),
        cam_hot,
    )
    pack(pre_c, [both[:16], both[16:]])
    table = all_sum(pre_c, pre_o, pre_p, 5)
    rhs = unpack(table, 0)
    precond = unpack(table, 1) + DAMPING

    def push(x):
        at_obs = gather(x, cam_hot)
        along_u = jnp.sum(slopes_u[...] * at_obs, axis=0, keepdims=True)
        along_v = jnp.sum(slopes_v[...] * at_obs, axis=0, keepdims=True)
        push_c[me[lead]] = to_points([land_u[i] * along_u + land_v[i] * along_v for i in range(3)])
        return along_u, along_v, members_of(all_sum(push_c, push_o, push_p, 8), 3)

    def dot(a, b):
        return jnp.sum(jnp.sum(a * b, axis=0, keepdims=True), axis=1, keepdims=True)

    def iterate(_, state):
        x, res, direction, rz, *sums = state
        along_u, along_v, pushed = push(direction)
        pulled_u, pulled_v = at_slots(solve(pushed))
        left_u, left_v = along_u - pulled_u, along_v - pulled_v
        pack(sum_c, [scatter(slopes_u[...] * left_u + slopes_v[...] * left_v, cam_hot)])
        image = unpack(all_sum(sum_c, sum_o, sum_p, 11), 0) + DAMPING * direction
        alpha = rz / dot(direction, image)
        x = x + alpha * direction
        sums = [sums[i] + alpha * pushed[i] for i in range(3)]
        res = res - alpha * image
        pre = res / precond
        rz_new = dot(res, pre)
        sent()
        return (x, res, pre + (rz_new / rz) * direction, rz_new, *sums)

    sent()
    pre = rhs / precond
    sums = [jnp.zeros_like(gradient[0])] * 3
    state = (jnp.zeros_like(rhs), rhs, pre, dot(rhs, pre), *sums)
    x, _, _, _, *pushed = lax.fori_loop(0, ITERS, iterate, state)
    full_x[...] = x
    at = pl.multiple_of(me["cam"] * cams_local, cams_local)
    cam_out[...] = full_x[0:9, pl.ds(at, cams_local)]
    steps = solve([-(gradient[i] + pushed[i]) for i in range(3)])
    for i in range(3):
        full_p[i] = steps[i]
        point_out[i : i + 1, :] = full_p[i, pl.ds(me["obs"], 1), :]


def local(cameras, points, measured, sqrt_weight, cam_index, point_slot, block_owner, valid_count):
    n_obs, n_cam = lax.axis_size("obs"), lax.axis_size("cam")
    slots = cam_index.shape[0] * cam_index.shape[1]
    pts_local, cams_local = points.shape[1], cameras.shape[1]
    cams_all = cams_local * n_cam
    one = ceil_to(9 * (cams_all // 128), 8)
    three, nine = ceil_to(3 * n_obs, 16), ceil_to(9 * n_obs, 16)

    flat, chips = by_chips(n_obs, n_cam), n_obs * n_cam // 2

    def pair(rows, columns):
        if not flat:
            return [pltpu.VMEM((n, rows, columns), F32) for n in (n_cam, n_obs)] + [
                pltpu.VMEM((1, 8, 128), F32)
            ]
        part = rows // 2
        return [
            pltpu.VMEM((2, rows, columns), F32),
            pltpu.VMEM((chips, part, columns), F32),
            pltpu.VMEM((2, part, columns), F32),
        ]

    vmem, smem = pl.BlockSpec(memory_space=pltpu.VMEM), pl.BlockSpec(memory_space=pltpu.SMEM)
    loaded = (cameras, points, measured, sqrt_weight, cam_index, point_slot)
    return pl.pallas_call(
        functools.partial(kernel, n_obs, n_cam),
        out_shape=(
            jax.ShapeDtypeStruct((9, cams_local), F32),
            jax.ShapeDtypeStruct((3, pts_local), F32),
        ),
        in_specs=[pl.BlockSpec(memory_space=pl.ANY)] * 6 + [vmem, smem],
        out_specs=(vmem, vmem),
        scratch_shapes=[
            pltpu.VMEM((n_cam, 16, cams_local), F32),
            pltpu.VMEM((n_obs, 8, pts_local), F32),
            *pair(nine, pts_local),
            *pair(2 * one, 128),
            *pair(three, pts_local),
            *pair(ceil_to(one, 16), 128),
            pltpu.VMEM((cams_all, slots), BF16),
            pltpu.VMEM((pts_local, slots), BF16),
            pltpu.VMEM((16, slots), F32),
            pltpu.VMEM((16, slots), F32),
            pltpu.VMEM((16, cams_all), F32),
            pltpu.VMEM((3, n_obs, pts_local), F32),
            pltpu.SemaphoreType.DMA((14, max(n_obs, n_cam, chips if flat else 0))),
            pltpu.SemaphoreType.DMA((14, max(n_obs, n_cam, chips if flat else 0))),
            pltpu.SemaphoreType.DMA((6,)),
            *[pltpu.VMEM(x.shape, x.dtype) for x in loaded],
        ],
        compiler_params=pltpu.CompilerParams(
            collective_id=0, has_side_effects=True, vmem_limit_bytes=48 * 1024 * 1024
        ),
    )(cameras, points, measured, sqrt_weight, cam_index, point_slot, block_owner, valid_count)


def solution(mesh):
    return jax.shard_map(
        local,
        mesh=mesh,
        in_specs=(
            P(None, ("groups", "cam")),
            P(None, ("groups", "obs")),
            P(("groups", "obs", "cam"), None, None),
            P(("groups", "obs", "cam"), None),
            P(("groups", "obs", "cam"), None),
            P(("groups", "obs", "cam"), None),
            P(("groups", "obs", "cam"), None),
            P(("groups", "obs", "cam")),
        ),
        out_specs=(P(None, ("groups", "cam")), P(None, ("groups", "obs"))),
        check_vma=False,
    )
```
